32 devices in a mesh: dp: 8 (over y, x, core), tensor: 4 (over z).
Axes of the slice: x: 2, y: 2, z: 4, core: 2. Of those that a mesh axis runs over, the one named last changes fastest.
Arguments:
- layer_input: bfloat16 [20480, 2048], P('dp', 'tensor'), may hold values from -6 to 6
- positions: int32 [20480], P('dp'), may hold values from -1 to 2559, as said below
- norm_first: bfloat16 [2048], P('tensor'), may hold values from 0.5 to 1.5
- w_query: bfloat16 [2048, 2048], P(None, 'tensor'), may hold values from -0.125 to 0.125
- w_key: bfloat16 [2048, 256], replicated, may hold values from -0.125 to 0.125
- w_value: bfloat16 [2048, 256], replicated, may hold values from -0.125 to 0.125
- w_out: bfloat16 [2048, 2048], P('tensor'), may hold values from -1.5 to 1.5
- norm_second: bfloat16 [2048], P('tensor'), may hold values from 0.5 to 1.5
- w_gate: bfloat16 [2048, 5632], P(None, 'tensor'), may hold values from -0.125 to 0.125
- w_up: bfloat16 [2048, 5632], P(None, 'tensor'), may hold values from -0.125 to 0.125
- w_down: bfloat16 [5632, 2048], P('tensor'), may hold values from -0.078125 to 0.078125
- cotangent: bfloat16 [20480, 2048], P('dp', 'tensor'), may hold values from -6 to 6
Outputs:
- mixed: bfloat16 [20480, 2048], P('dp', 'tensor')
- grad_input: float32 [20480, 2048], P('dp', 'tensor')
- grad_norm_first: float32 [2048], P(('dp', 'tensor'))
- grad_query: float32 [2048, 2048], P('dp', 'tensor')
- grad_key: float32 [2048, 256], P(('dp', 'tensor'))
- grad_value: float32 [2048, 256], P(('dp', 'tensor'))
- grad_out: float32 [2048, 2048], P('tensor', 'dp')
- grad_norm_second: float32 [2048], P(('dp', 'tensor'))
- grad_gate: float32 [2048, 5632], P('dp', 'tensor')
- grad_up: float32 [2048, 5632], P('dp', 'tensor')
- grad_down: float32 [5632, 2048], P('tensor', 'dp')
The draws below stay inside these ranges and needn't reach their ends.
Inputs may be any that keep to these rules, and one draw needn't show every extreme that they name: `positions`: each group of 2560 rows holds whole sequences of 1024 or more tokens laid end to end from its first row, numbered 0, 1, 2, ...; its unused rows follow them and hold -1. In every draw one group holds a single sequence of 2560 tokens, another group holds two or more sequences, and every group but the one with the single 2560-token sequence has unused rows.
All inputs are finite; a program needn't handle non-finite values.
Results may differ from the reference program's by a relative error of at most 0.024.
Values may be sent and summed in bfloat16 or wider, within the bound.
A program may use at most 576 MiB of HBM per device.

```python
import math
import jax
import jax.numpy as jnp
from jax import lax

D = 2048
H = 32
KV = 4
HD = 64
FF = 5632
CAP = 2560
MINLEN = 1024
QBLK = 512
TOKENS = 20480


def draw_positions(key, part):
    key = jax.random.fold_in(key, 7)
    groups = TOKENS // CAP
    most_cuts = max(CAP // MINLEN - 1, 1)
    key_full, key_pair, key_used, key_two, key_cuts = jax.random.split(key, 5)
    full_group = jax.random.randint(key_full, (), 0, groups)
    pair_group = (full_group + 1 + jax.random.randint(key_pair, (), 0, groups - 1)) % groups
    group_index = jnp.arange(groups)
    used_rows = jax.random.randint(key_used, (groups,), MINLEN, CAP)
    two_rows = jax.random.randint(key_two, (groups,), 2 * MINLEN, CAP)
    used_rows = jnp.where(group_index == pair_group, two_rows, used_rows)
    is_full = group_index == full_group
    used_rows = jnp.where(is_full, CAP, used_rows)
    seq_count = jnp.where(is_full, 1, used_rows // MINLEN)
    spare_rows = used_rows - seq_count * MINLEN
    raw_cuts = jax.random.randint(key_cuts, (groups, most_cuts), 0, 1 << 20)
    cut_points = jnp.sort(raw_cuts % (spare_rows[:, None] + 1), axis=1)
    cut_index = jnp.arange(most_cuts) + 1
    bounds = jnp.where(cut_index[None, :] < seq_count[:, None], cut_index[None, :] * MINLEN + cut_points, used_rows[:, None])
    bounds = jnp.concatenate([jnp.zeros((groups, 1), jnp.int32), bounds.astype(jnp.int32)], axis=1)
    row_index = jnp.arange(CAP)
    begins = jnp.max(jnp.where(bounds[:, None, :] <= row_index[None, :, None], bounds[:, None, :], 0), axis=2)
    places = jnp.where(row_index[None, :] < used_rows[:, None], row_index[None, :] - begins, -1)
    return places.reshape(-1).astype(jnp.int32)


def raised(array, key, source, target, blocks, factor):
    def block_of(position):
        return (jnp.arange(array.shape[position]) // (array.shape[position] // blocks)).reshape((-1,) + (1,) * (array.ndim - 1 - position))

    near = jax.random.permutation(key, blocks)[block_of(target)]
    far = (block_of(target) + blocks // 2) % blocks
    return jnp.where((block_of(source) == near) | (block_of(source) == far), factor * array, array)


def block_levels(own_key, extent, cuts, least, largest):
    def one(dim, shards_of):
        draws = jax.random.uniform(jax.random.fold_in(jax.random.fold_in(own_key, 6), dim), (shards_of,), jnp.float32, least / len(cuts), largest / len(cuts))
        return jnp.repeat(jnp.exp(draws), extent[dim] // shards_of).reshape((-1,) + (1,) * (len(extent) - dim - 1))

    factor_of = one(*cuts[0])
    for cut in cuts[1:]:
        factor_of = factor_of * one(*cut)
    return factor_of


def centred(stream_key, shape, scale, reach, pieces=(), kind=jnp.bfloat16):
    array = jax.random.normal(stream_key, shape, jnp.float32) * scale
    if len(pieces) > 0:
        array = block_levels(stream_key, shape, pieces, -0.22, 0.18) * array
    return jnp.clip(array, min=-reach, max=reach).astype(kind)


def noise_with(rng, extent, spread, most, cuts, heavy, kind=jnp.bfloat16):
    values = spread * jax.random.normal(rng, extent, jnp.float32)
    if cuts:
        values = values * block_levels(rng, extent, cuts, -0.22, 0.18)
    return jnp.clip(raised(values, jax.random.fold_in(rng, 3), *heavy), -most, most).astype(kind)


def setup_inputs(seed: int = 0) -> dict:
    key_list = jax.random.split(jax.random.key(seed), 13)
    return {
        "layer_input": centred(key_list[0], (TOKENS, D), 1.0, 6.0, ((0, 8), (1, 4))),
        "positions": draw_positions(jax.random.fold_in(key_list[12], 71), 0),
        "norm_first": jnp.clip(1.0 + 0.1 * jax.random.normal(key_list[2], (D,), jnp.float32), 0.5, 1.5).astype(jnp.bfloat16),
        "w_query": centred(key_list[3], (D, H * HD), D ** -0.5, 0.125, ((1, 4),)),
        "w_key": centred(key_list[4], (D, KV * HD), D ** -0.5, 0.125),
        "w_value": centred(key_list[5], (D, KV * HD), D ** -0.5, 0.125),
        "w_out": centred(key_list[6], (H * HD, D), (max(H * HD // 128, 1)) ** -0.5, 1.5, ((0, 4),)),
        "norm_second": jnp.clip(1.0 + 0.1 * jax.random.normal(key_list[7], (D,), jnp.float32), 0.5, 1.5).astype(jnp.bfloat16),
        "w_gate": centred(key_list[8], (D, FF), D ** -0.5, 0.125, ((1, 4),)),
        "w_up": centred(key_list[9], (D, FF), D ** -0.5, 0.125, ((1, 4),)),
        "w_down": centred(key_list[10], (FF, D), FF ** -0.5, 0.078125, ((0, 4),)),
        "cotangent": noise_with(key_list[11], (TOKENS, D), 1.0, 6.0, ((0, 8), (1, 4)), (0, 1, 8, 2.0)),
    }


EPS = 1e-05
MASKED = -1e+30
EXACT = lax.Precision.HIGHEST

@jax.custom_vjp
def low(v):
    return lax.optimization_barrier(v.astype(jnp.bfloat16)).astype(jnp.float32)

@jax.custom_vjp
def low_back(v):
    return v

def low_keep(v):
    return (low(v), None)

def low_pass(kept, grad):
    return (grad,)

def back_keep(v):
    return (v, None)

def back_low(kept, grad):
    return (low(grad),)
low.defvjp(low_keep, low_pass)
low_back.defvjp(back_keep, back_low)

def matmul(left_side, right_side):
    return jnp.dot(left_side, right_side, precision=EXACT)

def rotate(values, places, direction):
    half_dim = values.shape[-1] // 2
    frequency = 10000.0 ** (-(jnp.arange(half_dim, dtype=jnp.float32) * 2.0 / values.shape[-1]))
    angles = places.astype(jnp.float32)[:, None] * frequency[None, :]
    cosine = jnp.cos(angles)[:, None, :]
    sines = direction * jnp.sin(angles)[:, None, :]
    front_half = values[..., :half_dim]
    back_half = values[..., half_dim:]
    return jnp.concatenate([front_half * cosine - back_half * sines, back_half * cosine + front_half * sines], axis=-1)

def attention(queries, key_rows, value_rows, places):
    blocks = CAP // QBLK
    key_index = jnp.arange(CAP, dtype=jnp.int32)
    score_scale = 1.0 / math.sqrt(HD)

    def one_block(block_index):
        first_row = block_index * QBLK
        block_queries = lax.dynamic_slice_in_dim(queries, first_row, QBLK, 0)
        block_places = lax.dynamic_slice_in_dim(places, first_row, QBLK, 0)
        rows_here = first_row + jnp.arange(QBLK, dtype=jnp.int32)
        scores = jnp.einsum('qkgd,ckgd->qkgc', block_queries, key_rows, precision=EXACT) * score_scale
        scores = low_back(scores)
        visible = (key_index[None, :] <= rows_here[:, None]) & (places[None, :] >= 0)
        visible = visible & (block_places[:, None] - places[None, :] == rows_here[:, None] - key_index[None, :])
        visible = visible | (key_index[None, :] == rows_here[:, None])
        scores = jnp.where(visible[:, None, None, :], scores, MASKED)
        row_top = lax.optimization_barrier(jnp.max(scores, axis=-1, keepdims=True))
        weights = jnp.exp(scores - row_top)
        probabilities = low(weights / lax.optimization_barrier(jnp.sum(weights, axis=-1, keepdims=True)))
        return jnp.einsum('qkgc,ckgd->qkgd', probabilities, value_rows, precision=EXACT)
    results = lax.map(jax.checkpoint(one_block), jnp.arange(blocks, dtype=jnp.int32))
    return results.reshape(CAP, H * HD)

def group_forward(params, group_rows, places):
    gain_first, w_query, w_key, w_value, w_out, gain_second, w_gate, w_up, w_down = params
    share = H // KV
    scale_first = lax.rsqrt(lax.optimization_barrier(jnp.mean(group_rows * group_rows, axis=-1, keepdims=True)) + EPS)
    normed_first = low(group_rows * scale_first * gain_first)
    query_lin = low_back(matmul(normed_first, w_query)).reshape(CAP, H, HD)
    queries = low(rotate(query_lin, places, 1.0)).reshape(CAP, KV, share, HD)
    key_lin = jnp.broadcast_to(matmul(normed_first, w_key).reshape(CAP, KV, 1, HD), (CAP, KV, share, HD))
    key_lin = low_back(key_lin).reshape(CAP, H, HD)
    key_rows = low(rotate(key_lin, places, 1.0)).reshape(CAP, KV, share, HD)
    value_lin = jnp.broadcast_to(matmul(normed_first, w_value).reshape(CAP, KV, 1, HD), (CAP, KV, share, HD))
    value_rows = low(low_back(value_lin))
    attended = low(low_back(attention(queries, key_rows, value_rows, places)))
    residual = group_rows + low_back(matmul(attended, w_out))
    scale_second = lax.rsqrt(lax.optimization_barrier(jnp.mean(residual * residual, axis=-1, keepdims=True)) + EPS)
    normed_second = low(residual * scale_second * gain_second)
    gate_act = low_back(matmul(normed_second, w_gate))
    upward = low_back(matmul(normed_second, w_up))
    hidden = low(jax.nn.silu(gate_act) * upward)
    return residual + matmul(hidden, w_down)

def reference(layer_input, positions, norm_first, w_query, w_key, w_value, w_out, norm_second, w_gate, w_up, w_down, cotangent):
    params = tuple((weight.astype(jnp.float32) for weight in (norm_first, w_query, w_key, w_value, w_out, norm_second, w_gate, w_up, w_down)))
    groups = layer_input.shape[0] // CAP
    grouped = (layer_input.astype(jnp.float32).reshape(groups, CAP, D), positions.reshape(groups, CAP), cotangent.astype(jnp.float32).reshape(groups, CAP, D))

    def per_group(totals, group_item):
        group_rows, places, incoming = group_item
        result, pullback = jax.vjp(lambda weights, inputs: group_forward(weights, inputs, places), params, group_rows)
        weight_grads, input_grads = pullback(incoming)
        totals = jax.tree.map(lambda summed, added: summed + added, totals, weight_grads)
        return (totals, (result.astype(jnp.bfloat16), input_grads))
    zero_grads = jax.tree.map(jnp.zeros_like, params)
    totals, (mixed, grad_input) = lax.scan(per_group, zero_grads, grouped)
    return (mixed.reshape(-1, D), grad_input.reshape(-1, D), totals[0], totals[1], totals[2], totals[3], totals[4], totals[5], totals[6], totals[7], totals[8])
```

```python
import functools

import jax
import jax.numpy as jnp
from jax import lax
from jax.experimental import pallas as pl
from jax.experimental.pallas import tpu as pltpu
from jax.sharding import PartitionSpec as P

HD = 64
EPS = 1e-05
MASKED = -1e30
NB = 5
KC = 256
SUM_ROWS = 16
F32 = jnp.float32
BF16 = jnp.bfloat16


def mm(left, right, dims):
    return lax.dot_general(left, right, ((dims[0], dims[1]), ((), ())), preferred_element_type=F32)


def spans(bounds_ref, r):
    return tuple(bounds_ref[r, i] for i in range(4))


def forward_kernel(bounds_ref, q_ref, lo_ref, hi_ref, k_ref, vt_ref, o_ref, lse_ref, acc_ref, top_ref):
    r = pl.program_id(1)
    share = q_ref.shape[1] // HD
    width = q_ref.shape[2]
    pairs = share // 2
    first, full_first, full_last, last = spans(bounds_ref, r)
    low = lo_ref[0]
    high = hi_ref[0]
    low2 = jnp.concatenate([low, low], axis=1)
    high2 = jnp.concatenate([high, high], axis=1)
    acc_ref[...] = jnp.zeros_like(acc_ref)
    top_ref[...] = jnp.full_like(top_ref, MASKED)

    def chunk(c, masked):
        keys = k_ref[0, pl.ds(pl.multiple_of(c * KC, KC), KC), :]
        values_t = vt_ref[0, c]
        if masked:
            index = lax.broadcasted_iota(jnp.int32, (KC, 2 * width), 0) + c * KC
            visible = (index >= low2) & (index <= high2)
        for p in range(pairs):
            queries = jnp.concatenate(
                [q_ref[0, (2 * p) * HD : (2 * p + 1) * HD, :], q_ref[0, (2 * p + 1) * HD : (2 * p + 2) * HD, :]], axis=1
            )
            scores = mm(keys, queries, ((1,), (0,)))
            if masked:
                scores = jnp.where(visible, scores, MASKED)
            old = top_ref[p]
            top = jnp.maximum(old, jnp.max(scores, axis=0, keepdims=True))
            weights = jnp.exp(scores - top).astype(BF16)
            top_ref[p] = top
            acc_ref[p] = acc_ref[p] * jnp.exp(old - top) + mm(values_t, weights, ((1,), (0,)))

    @pl.loop(full_first, full_last)
    def _(c):
        chunk(c, False)

    @pl.loop(0, (full_first - first) + (last - full_last))
    def _(t):
        before = full_first - first
        chunk(jnp.where(t < before, first + t, full_last + t - before), True)

    for p in range(pairs):
        acc = acc_ref[p]
        total = acc[HD : HD + 1, :]
        out = acc[:HD, :] / total
        logs = top_ref[p] + jnp.log(total)
        for side in range(2):
            h = 2 * p + side
            cols = slice(side * width, (side + 1) * width)
            o_ref[0, h * HD : (h + 1) * HD, :] = out[:, cols].astype(BF16)
            lse_ref[0, 0, h : h + 1, :] = logs[:, cols]


def backward_kernel(
    bounds_ref, q_ref, do_ref, o_ref, lse_ref, lo_ref, hi_ref, k_ref, v_ref, kt_ref, dq_ref, dk_ref, dv_ref, acc_ref
):
    r = pl.program_id(1)
    share = q_ref.shape[1] // HD
    width = q_ref.shape[2]
    pairs = share // 2
    first, full_first, full_last, last = spans(bounds_ref, r)
    low = lo_ref[0]
    high = hi_ref[0]
    low2 = jnp.concatenate([low, low], axis=1)
    high2 = jnp.concatenate([high, high], axis=1)

    @pl.when(r == 0)
    def _():
        dk_ref[...] = jnp.zeros_like(dk_ref)
        dv_ref[...] = jnp.zeros_like(dv_ref)

    acc_ref[...] = jnp.zeros_like(acc_ref)

    def both(ref, p):
        return jnp.concatenate(
            [ref[0, (2 * p) * HD : (2 * p + 1) * HD, :], ref[0, (2 * p + 1) * HD : (2 * p + 2) * HD, :]], axis=1
        )

    stats = []
    for p in range(pairs):
        logs = jnp.concatenate([lse_ref[0, 0, 2 * p : 2 * p + 1, :], lse_ref[0, 0, 2 * p + 1 : 2 * p + 2, :]], axis=1)
        delta = jnp.sum(both(do_ref, p).astype(F32) * both(o_ref, p).astype(F32), axis=0, keepdims=True)
        stats.append((logs, delta))

    def chunk(c, masked):
        rows = pl.ds(pl.multiple_of(c * KC, KC), KC)
        keys = k_ref[0, rows, :]
        values = v_ref[0, rows, :]
        keys_t = kt_ref[0, c]
        if masked:
            index = lax.broadcasted_iota(jnp.int32, (KC, 2 * width), 0) + c * KC
            visible = (index >= low2) & (index <= high2)
        sum_k = jnp.zeros((KC, HD), F32)
        sum_v = jnp.zeros((KC, HD), F32)
        for p in range(pairs):
            queries = both(q_ref, p)
            douts = both(do_ref, p)
            logs, delta = stats[p]
            probs = jnp.exp(mm(keys, queries, ((1,), (0,))) - logs)
            if masked:
                probs = jnp.where(visible, probs, 0.0)
            dprobs = mm(values, douts, ((1,), (0,)))
            dscores = (probs * (dprobs - delta)).astype(BF16)
            sum_v = sum_v + mm(probs.astype(BF16), douts, ((1,), (1,)))
            sum_k = sum_k + mm(dscores, queries, ((1,), (1,)))
            acc_ref[p] += mm(keys_t, dscores, ((1,), (0,)))
        dk_ref[0, rows, :] += sum_k
        dv_ref[0, rows, :] += sum_v

    @pl.loop(full_first, full_last)
    def _(c):
        chunk(c, False)

    @pl.loop(0, (full_first - first) + (last - full_last))
    def _(t):
        before = full_first - first
        chunk(jnp.where(t < before, first + t, full_last + t - before), True)

    for p in range(pairs):
        for side in range(2):
            h = 2 * p + side
            dq_ref[0, h * HD : (h + 1) * HD, :] = acc_ref[p, :, side * width : (side + 1) * width]


def attend(bounds, q_t, lows, highs, keys, values_t):
    kv, capacity = keys.shape[0], keys.shape[1]
    blocks, wide, width = q_t.shape
    slab = wide // kv
    share = slab // HD
    work = kv * share * blocks * width * capacity // 2
    return pl.pallas_call(
        forward_kernel,
        out_shape=(
            jax.ShapeDtypeStruct((blocks, wide, width), BF16),
            jax.ShapeDtypeStruct((blocks, kv, share, width), F32),
        ),
        grid_spec=pltpu.PrefetchScalarGridSpec(
            num_scalar_prefetch=1,
            grid=(kv, blocks),
            in_specs=[
                pl.BlockSpec((1, slab, width), lambda m, r, b: (r, m, 0)),
                pl.BlockSpec((1, 1, width), lambda m, r, b: (r, 0, 0)),
                pl.BlockSpec((1, 1, width), lambda m, r, b: (r, 0, 0)),
                pl.BlockSpec((1, capacity, HD), lambda m, r, b: (m, 0, 0)),
                pl.BlockSpec((1, capacity // KC, HD + SUM_ROWS, KC), lambda m, r, b: (m, 0, 0, 0)),
            ],
            out_specs=[
                pl.BlockSpec((1, slab, width), lambda m, r, b: (r, m, 0)),
                pl.BlockSpec((1, 1, share, width), lambda m, r, b: (r, m, 0, 0)),
            ],
            scratch_shapes=[
                pltpu.VMEM((share // 2, HD + SUM_ROWS, 2 * width), F32),
                pltpu.VMEM((share // 2, 1, 2 * width), F32),
            ],
        ),
        compiler_params=pltpu.CompilerParams(vmem_limit_bytes=32 * 1024 * 1024),
        cost_estimate=pl.CostEstimate(flops=4 * work * HD * 4, bytes_accessed=12 * 1024 * 1024, transcendentals=work),
        name="attention_forward",
    )(bounds, q_t, lows, highs, keys, values_t)


def attend_back(bounds, q_t, do_t, o_t, lse, lows, highs, keys, values, keys_t):
    kv, capacity = keys.shape[0], keys.shape[1]
    blocks, wide, width = q_t.shape
    slab = wide // kv
    share = slab // HD
    work = kv * share * blocks * width * capacity // 2
    slab_spec = pl.BlockSpec((1, slab, width), lambda m, r, b: (r, m, 0))
    row_spec = pl.BlockSpec((1, 1, width), lambda m, r, b: (r, 0, 0))
    key_spec = pl.BlockSpec((1, capacity, HD), lambda m, r, b: (m, 0, 0))
    return pl.pallas_call(
        backward_kernel,
        out_shape=(
            jax.ShapeDtypeStruct((blocks, wide, width), F32),
            jax.ShapeDtypeStruct((kv, capacity, HD), F32),
            jax.ShapeDtypeStruct((kv, capacity, HD), F32),
        ),
        grid_spec=pltpu.PrefetchScalarGridSpec(
            num_scalar_prefetch=1,
            grid=(kv, blocks),
            in_specs=[
                slab_spec,
                slab_spec,
                slab_spec,
                pl.BlockSpec((1, 1, share, width), lambda m, r, b: (r, m, 0, 0)),
                row_spec,
                row_spec,
                key_spec,
                key_spec,
                pl.BlockSpec((1, capacity // KC, HD, KC), lambda m, r, b: (m, 0, 0, 0)),
            ],
            out_specs=[slab_spec, key_spec, key_spec],
            scratch_shapes=[pltpu.VMEM((share // 2, HD, 2 * width), F32)],
        ),
        compiler_params=pltpu.CompilerParams(vmem_limit_bytes=32 * 1024 * 1024),
        cost_estimate=pl.CostEstimate(flops=10 * work * HD * 4, bytes_accessed=24 * 1024 * 1024, transcendentals=work),
        name="attention_backward",
    )(bounds, q_t, do_t, o_t, lse, lows, highs, keys, values, keys_t)


def shift(array, size, step):
    return lax.ppermute(array, "tensor", [(i, (i + step) % size) for i in range(size)])


def swap(array, size, bit):
    return lax.ppermute(array, "dp", [(i, i ^ (1 << bit)) for i in range(size)])


def pick(stack, index):
    return lax.dynamic_index_in_dim(stack, index, 0, keepdims=False)


def by_owner(array, size):
    width = array.shape[0] // (NB * size)
    grid = array.reshape(NB, size, width, array.shape[1])
    turned = jnp.stack([grid[r] if r % 2 == 0 else grid[r, ::-1] for r in range(NB)], axis=1)
    return turned.reshape(size, NB * width, array.shape[1])


def by_place(stack):
    size, rows, features = stack.shape
    grid = stack.reshape(size, NB, rows // NB, features)
    turned = jnp.stack([grid[:, r] if r % 2 == 0 else grid[::-1, r] for r in range(NB)], axis=0)
    return turned.reshape(size * rows, features)


def exchange(stack, rank):
    size = stack.shape[0]
    parts = [pick(stack, rank)]
    for step in range(1, size):
        parts.append(shift(pick(stack, lax.rem(rank + step, size)), size, step))
    ahead = [parts[(size - j) % size] for j in range(size)]
    both = jnp.stack(ahead + ahead[: size - 1], axis=0)
    return lax.dynamic_slice_in_dim(both, lax.rem(size - rank, size), size, 0)


def to_rows(array, size, rank):
    got = exchange(by_owner(array, size), rank)
    return got.transpose(1, 0, 2).reshape(got.shape[1], -1)


def to_features(array, size, rank):
    rows = array.shape[0]
    stack = array.reshape(rows, size, -1).transpose(1, 0, 2)
    return by_place(exchange(stack, rank))


def gather_shards(shard, dim, dp_size, dp_rank, size):
    length = shard.shape[dim] // dp_size
    piece = lax.dynamic_slice_in_dim(shard, dp_rank * length, length, dim)
    shards = [shard]
    for step in range(1, size):
        far = shift(piece, size, size - step)
        shards.append(lax.all_gather(far, "dp", axis=dim, tiled=True))
    return shards


def scatter_blocks(make, dp_size, dp_rank):
    bits = dp_size.bit_length() - 1
    core = dp_rank % 2
    evens = 2 * jnp.arange(dp_size // 2)
    away = swap(make(evens + (1 - core)).astype(BF16), dp_size, 0)
    near = make(evens + core) + away.astype(F32)
    half = near.shape[1] // 2
    done = []
    for part in range(2):
        total = near[:, part * half : (part + 1) * half]
        order = list(range(1, bits))
        if part == 1 and len(order) > 1:
            order[0], order[1] = order[1], order[0]
        left = list(range(1, bits))
        for bit in order:
            place = left.index(bit)
            shape = (2 ** (len(left) - 1 - place), 2, 2**place) + total.shape[1:]
            split = total.reshape(shape)
            mine = (dp_rank >> bit) & 1
            keep = lax.dynamic_index_in_dim(split, mine, 1, keepdims=False)
            send = lax.dynamic_index_in_dim(split, 1 - mine, 1, keepdims=False)
            got = swap(send.astype(BF16), dp_size, bit)
            total = (keep + got.astype(F32)).reshape((-1,) + total.shape[1:])
            left.remove(bit)
        done.append(total[0])
    return jnp.concatenate(done, axis=0)


def scatter_shards(partials, size):
    total = partials[0]
    for step in range(1, size):
        total = total + shift(partials[step].astype(BF16), size, step).astype(F32)
    return total


def turn(values_t, cosine, sine):
    half = HD // 2
    front, back = values_t[:, :half], values_t[:, half:]
    return jnp.concatenate([front * cosine - back * sine, back * cosine + front * sine], axis=1)


def rolled(parts, rank):
    size = len(parts)
    both = jnp.concatenate(parts + parts[: size - 1], axis=0)
    length = parts[0].shape[0]
    return lax.dynamic_slice_in_dim(both, lax.rem(size - rank, size) * length, size * length, 0)


def local(
    layer_input, positions, norm_first, w_query, w_key, w_value, w_out, norm_second, w_gate, w_up, w_down, cotangent
):
    size = lax.axis_size("tensor")
    rank = lax.axis_index("tensor")
    dp_size = lax.axis_size("dp")
    dp_rank = lax.axis_index("dp")
    capacity = layer_input.shape[0]
    width = w_key.shape[0]
    kv = w_key.shape[1] // HD
    rows = capacity // size
    block = rows // NB
    heads = w_query.shape[1] * size // HD
    hidden = w_gate.shape[1]

    gain_first = lax.all_gather(norm_first, "tensor", axis=0, tiled=True).astype(F32)
    gain_second = lax.all_gather(norm_second, "tensor", axis=0, tiled=True).astype(F32)

    x_low = to_rows(layer_input, size, rank)
    own_ids = jnp.stack([r * size + (rank if r % 2 == 0 else size - 1 - rank) for r in range(NB)])
    place_blocks = positions.reshape(NB * size, block)
    own_places = jnp.concatenate([pick(place_blocks, own_ids[r])[None] for r in range(NB)], axis=0)
    own_index = own_ids[:, None] * block + jnp.arange(block, dtype=jnp.int32)[None, :]
    lows = own_index - jnp.maximum(own_places, 0)
    most, least = jnp.max(lows, axis=1), jnp.min(lows, axis=1)
    last = (own_ids * block + block + KC - 1) // KC
    first = least // KC
    full_first = jnp.minimum((most + KC - 1) // KC, last)
    full_last = jnp.clip((own_ids * block + 1) // KC, full_first, last)
    bounds = jnp.stack([first, full_first, full_last, last], axis=1).astype(jnp.int32)
    lows = lows[:, None, :]
    highs = own_index[:, None, :]

    frequency = 10000.0 ** (-(jnp.arange(HD // 2, dtype=F32) * 2.0 / HD))
    angles = own_places.reshape(1, rows).astype(F32) * frequency[:, None]
    cosine, sine = jnp.cos(angles), jnp.sin(angles)

    query_w = gather_shards(w_query, 0, dp_size, dp_rank, size)
    out_w = gather_shards(w_out, 0, dp_size, dp_rank, size)
    gate_up = jnp.concatenate([w_gate, w_up], axis=1)
    gate_up_w = gather_shards(gate_up, 0, dp_size, dp_rank, size)
    down_w = gather_shards(w_down, 0, dp_size, dp_rank, size)

    x_rows = x_low.astype(F32)
    scale_first = lax.rsqrt(jnp.mean(x_rows * x_rows, axis=1, keepdims=True) + EPS)
    xn1 = (x_rows * scale_first * gain_first).astype(BF16)
    key_t = mm(w_key, xn1, ((0,), (1,)))
    key_rows = turn(key_t.reshape(kv, HD, rows), cosine, sine).reshape(kv * HD, rows).astype(BF16).T
    value_rows = mm(xn1, w_value, ((1,), (0,))).astype(BF16)
    own_kv = jnp.concatenate([key_rows, value_rows], axis=1)
    all_kv = by_place(
        jnp.stack([own_kv] * size) if size == 1 else lax.all_gather(own_kv, "tensor", axis=0, tiled=False)
    )
    keys = all_kv[:, : kv * HD].reshape(capacity, kv, HD).transpose(1, 0, 2)
    values = all_kv[:, kv * HD :].reshape(capacity, kv, HD).transpose(1, 0, 2)

    def chunked_t(array):
        return array.reshape(kv, capacity // KC, KC, HD).transpose(0, 1, 3, 2)

    keys_t = chunked_t(keys)
    ones = jnp.ones((kv, capacity // KC, SUM_ROWS, KC), BF16)
    values_t = jnp.concatenate([chunked_t(values), ones], axis=2)

    def to_blocks(array_t):
        return array_t.reshape(array_t.shape[0], NB, block).transpose(1, 0, 2)

    def from_blocks(blocks_t):
        return blocks_t.transpose(1, 0, 2).reshape(blocks_t.shape[1], rows)

    q_lin_t = rolled([mm(w, xn1, ((0,), (1,))) for w in query_w], rank)
    q_t = (turn(q_lin_t.reshape(heads, HD, rows), cosine, sine) * 0.125).reshape(heads * HD, rows).astype(BF16)
    q_t = to_blocks(q_t)
    o_blocks, lse = attend(bounds, q_t, lows, highs, keys, values_t)
    o_t = from_blocks(o_blocks)
    own_slab = heads * HD // size
    o_parts = [
        lax.dynamic_slice_in_dim(o_t, lax.rem(rank + k, size) * own_slab, own_slab, 0) for k in range(size)
    ]
    h = x_rows
    for k in range(size):
        h = h + mm(o_parts[k], out_w[k], ((0,), (0,)))

    scale_second = lax.rsqrt(jnp.mean(h * h, axis=1, keepdims=True) + EPS)
    xn2 = (h * scale_second * gain_second).astype(BF16)
    y = to_rows(cotangent, size, rank)
    result = h
    a_parts, gu_parts = [], []
    for k in range(size):
        gate_act_up = mm(xn2, gate_up_w[k], ((1,), (0,)))
        gate_act, upward = gate_act_up[:, :hidden], gate_act_up[:, hidden:]
        a_parts.append((gate_act * jax.nn.sigmoid(gate_act) * upward).astype(BF16))
        gu_parts.append(gate_act_up.astype(BF16))
    for k in range(size):
        result = result + mm(a_parts[k], down_w[k], ((1,), (0,)))
    mixed = to_features(result.astype(BF16), size, rank)

    def split_cols(array):
        return array.reshape(rows, dp_size, width // dp_size).transpose(1, 0, 2)

    def block_rows(source, other):
        stacks = split_cols(source)

        def make(index):
            chosen = stacks[index]
            return lax.dot_general(chosen, other, (((1,), (0,)), ((), ())), preferred_element_type=F32)

        return make

    d_parts = []
    for k in range(size):
        da = mm(y, down_w[k], ((1,), (1,)))
        gate_act = gu_parts[k][:, :hidden].astype(F32)
        upward = gu_parts[k][:, hidden:].astype(F32)
        sig = jax.nn.sigmoid(gate_act)
        d_gate = (da * upward * sig * (1.0 + gate_act * (1.0 - sig))).astype(BF16)
        d_up = (da * gate_act * sig).astype(BF16)
        d_parts.append(jnp.concatenate([d_gate, d_up], axis=1))
    grad_down = scatter_shards([scatter_blocks(block_rows(y, a), dp_size, dp_rank) for a in a_parts], size).T
    dxn2 = jnp.zeros((rows, width), F32)
    for k in range(size):
        dxn2 = dxn2 + mm(d_parts[k], gate_up_w[k], ((1,), (1,)))
    grad_gate_up = scatter_shards([scatter_blocks(block_rows(xn2, d), dp_size, dp_rank) for d in d_parts], size)
    scaled = dxn2 * gain_second
    stat_second = jnp.sum(scaled * h, axis=1, keepdims=True)
    dh = y.astype(F32) + scaled * scale_second - h * (scale_second**3 * stat_second / width)
    gain_two = jnp.sum(dxn2 * h * scale_second, axis=0)
    dhb = dh.astype(BF16)

    do_t = to_blocks(rolled([mm(w, dhb, ((1,), (1,))).astype(BF16) for w in out_w], rank))
    dq_blocks, d_keys, d_values = attend_back(bounds, q_t, do_t, o_blocks, lse, lows, highs, keys, values, keys_t)

    def block_rows_t(source, other_t):
        stacks = split_cols(source)

        def make(index):
            chosen = stacks[index]
            return lax.dot_general(chosen, other_t, (((1,), (1,)), ((), ())), preferred_element_type=F32)

        return make

    grad_out = scatter_shards([scatter_blocks(block_rows_t(dhb, o), dp_size, dp_rank) for o in o_parts], size).T
    d_kv = jnp.concatenate(
        [
            d_keys.transpose(1, 0, 2).reshape(capacity, kv * HD),
            d_values.transpose(1, 0, 2).reshape(capacity, kv * HD),
        ],
        axis=1,
    ).astype(BF16)
    own_dkv = jnp.sum(exchange(by_owner(d_kv, size), rank).astype(F32), axis=0)
    dk_lin = (
        turn(own_dkv[:, : kv * HD].T.reshape(kv, HD, rows), cosine, -sine).reshape(kv * HD, rows).T.astype(BF16)
    )
    dv_lin = own_dkv[:, kv * HD :].astype(BF16)
    dq_t = from_blocks(dq_blocks).reshape(heads, HD, rows) * 0.125
    dq_t = turn(dq_t, cosine, -sine).reshape(heads * HD, rows).astype(BF16)
    dq_parts = [
        lax.dynamic_slice_in_dim(dq_t, lax.rem(rank + k, size) * own_slab, own_slab, 0) for k in range(size)
    ]
    dxn1 = mm(dk_lin, w_key, ((1,), (1,))) + mm(dv_lin, w_value, ((1,), (1,)))
    for k in range(size):
        dxn1 = dxn1 + mm(dq_parts[k], query_w[k], ((0,), (1,)))
    scaled = dxn1 * gain_first
    stat_first = jnp.sum(scaled * x_rows, axis=1, keepdims=True)
    dx = dh + scaled * scale_first - x_rows * (scale_first**3 * stat_first / width)
    grad_input = to_features(dx.astype(BF16), size, rank).astype(F32)
    gain_one = jnp.sum(dxn1 * x_rows * scale_first, axis=0)

    grad_query = scatter_shards([scatter_blocks(block_rows_t(xn1, d), dp_size, dp_rank) for d in dq_parts], size)
    kv_block = scatter_blocks(block_rows(xn1, jnp.concatenate([dk_lin, dv_lin], axis=1)), dp_size, dp_rank)
    kv_stack = kv_block.astype(BF16).reshape(size, kv_block.shape[0] // size, kv_block.shape[1])
    grad_kv = jnp.sum(exchange(kv_stack, rank).astype(F32), axis=0)
    gains = lax.psum_scatter(jnp.stack([gain_one, gain_two], axis=1), ("dp", "tensor"), scatter_dimension=0, tiled=True)

    return (
        mixed,
        grad_input,
        gains[:, 0],
        grad_query,
        grad_kv[:, : kv * HD],
        grad_kv[:, kv * HD :],
        grad_out,
        gains[:, 1],
        grad_gate_up[:, :hidden],
        grad_gate_up[:, hidden:],
        grad_down,
    )


def solution(mesh):
    return jax.shard_map(
        local,
        mesh=mesh,
        in_specs=(
            P("dp", "tensor"),
            P("dp"),
            P("tensor"),
            P(None, "tensor"),
            P(),
            P(),
            P("tensor", None),
            P("tensor"),
            P(None, "tensor"),
            P(None, "tensor"),
            P("tensor", None),
            P("dp", "tensor"),
        ),
        out_specs=(
            P("dp", "tensor"),
            P("dp", "tensor"),
            P(("dp", "tensor")),
            P("dp", "tensor"),
            P(("dp", "tensor"), None),
            P(("dp", "tensor"), None),
            P("tensor", "dp"),
            P(("dp", "tensor")),
            P("dp", "tensor"),
            P("dp", "tensor"),
            P("tensor", "dp"),
        ),
        check_vma=False,
    )
```
